128 devices in a mesh: rows: 8 (over z, x_lo), vocab: 16 (over x_hi, y, core).
Axes of the slice: x: 4 (x_hi: 2, x_lo: 2; x = x_hi * 2 + x_lo), y: 4, z: 4, core: 2. Of those that a mesh axis runs over, the one named last changes fastest.
Arguments:
- hidden: bfloat16 [4096, 4096], P('rows', 'vocab')
- lexicon_projection_weights: bfloat16 [4096, 38912], P(None, 'vocab')
- sampled: int32 [4096], P('rows'), may hold values from 0 to 38911, as said below
- keep_bits: int32 [4096, 16], P('rows', 'vocab'), may hold values from 0 to 524287, as said below
Outputs:
- full_logprob: float32 [4096], P('rows')
- retained_log_chance: float32 [4096], P('rows')
- mean_gap: float32 [], replicated
The draws below stay inside these ranges and needn't reach their ends.
Inputs may be any that keep to these rules, and one draw needn't show every extreme that they name: sampled[t] is kept: its keep block's bit is set in keep_bits of its row. `keep_bits`: only the lowest 19 bits are used.
All inputs are finite; a program needn't handle non-finite values.
Results may differ from the reference program's by a relative error of at most 0.0003.
Values may be sent and summed in bfloat16 or wider, within the bound.
A program may use at most 128 MiB of HBM per device.

```python
import math
import jax
import jax.numpy as jnp
from jax import lax

D = 4096
VS_DEV = 2432
VBLK = 128
NBLK = 19
V = 38912
TOKENS = 4096
N_VOCAB = 16


def shared_weight(key):
    key = jax.random.fold_in(key, 101)
    first, second = jax.random.split(key)
    base = jax.random.normal(first, (D, V), jnp.float32) / math.sqrt(D)
    scales = jnp.exp(jax.random.uniform(second, (V,), jnp.float32, math.log(0.5), math.log(4.0)))
    return (base, scales)


def shared_tokens(key):
    return jax.random.randint(jax.random.fold_in(key, 202), (TOKENS,), 0, V, dtype=jnp.int32)


def draw_lexicon_projection_weights(key, part):
    base, scales = shared_weight(key)
    return (base * scales[None, :]).astype(jnp.bfloat16)


def draw_sampled(key, part):
    return shared_tokens(key)


def draw_keep_bits(key, part):
    tokens = shared_tokens(key)
    key = jax.random.fold_in(key, 3)
    first, second, third = jax.random.split(key, 3)
    top = 2 ** NBLK
    bits = jax.random.randint(first, (TOKENS, N_VOCAB), 0, top, dtype=jnp.int32)
    more = jax.random.randint(second, (TOKENS, N_VOCAB), 0, top, dtype=jnp.int32)
    most = jax.random.randint(third, (TOKENS, N_VOCAB), 0, top, dtype=jnp.int32)
    level = 1 + 3 * jnp.arange(TOKENS, dtype=jnp.int32) // TOKENS
    bits = jnp.where(level[:, None] >= 2, bits & more, bits)
    bits = jnp.where(level[:, None] >= 3, bits & most, bits)
    owner = tokens // VS_DEV
    position = tokens % VS_DEV // VBLK
    added = jnp.where(jnp.arange(N_VOCAB, dtype=jnp.int32)[None, :] == owner[:, None], jnp.left_shift(jnp.ones_like(position), position)[:, None], 0)
    bits = bits | added
    bits = jnp.where(jnp.arange(TOKENS, dtype=jnp.int32)[:, None] == 0, top - 1, bits)
    return bits


def draw_hidden(key, part):
    key = jax.random.fold_in(key, 5)
    first = jax.random.fold_in(key, 0)
    rows = jax.random.normal(first, (TOKENS, D), jnp.float32)
    return rows.astype(jnp.bfloat16)


def setup_inputs(seed: int = 0) -> dict:
    arg_keys = jax.random.split(jax.random.key(seed), 5)
    return {
        "hidden": draw_hidden(jax.random.fold_in(arg_keys[4], 71), 0),
        "lexicon_projection_weights": draw_lexicon_projection_weights(jax.random.fold_in(arg_keys[4], 71), 0),
        "sampled": draw_sampled(jax.random.fold_in(arg_keys[4], 71), 0),
        "keep_bits": draw_keep_bits(jax.random.fold_in(arg_keys[4], 71), 0),
    }


softness_divisor = 0.7


def reference(hidden, lexicon_projection_weights, sampled, keep_bits):
    block_rows = math.gcd(TOKENS, 512)
    count = TOKENS // block_rows
    shift_amounts = jnp.arange(NBLK, dtype=jnp.int32)

    def one_block(items):
        feature_slab_segment, rows_s, rows_k = items
        raw_preference_values = jnp.dot(feature_slab_segment, lexicon_projection_weights, preferred_element_type=jnp.float32) / softness_divisor
        columns = lax.broadcasted_iota(jnp.int32, raw_preference_values.shape, 1)
        picked = jnp.sum(jnp.where(columns == rows_s[:, None], raw_preference_values, 0.0), axis=1)
        blocks = jnp.right_shift(rows_k[:, :, None], shift_amounts[None, None, :]) & 1
        keep = jnp.broadcast_to(blocks[:, :, :, None], (block_rows, N_VOCAB, NBLK, VBLK)).reshape(block_rows, V).astype(jnp.int32)
        full_top = jnp.max(raw_preference_values, axis=1)
        full_lse = full_top + jnp.log(jnp.sum(jnp.exp(raw_preference_values - full_top[:, None]), axis=1))
        masked = jnp.where(keep == 1, raw_preference_values, -jnp.inf)
        kept_top = jnp.max(masked, axis=1)
        kept_lse = kept_top + jnp.log(jnp.sum(jnp.exp(masked - kept_top[:, None]), axis=1))
        return picked - full_lse, picked - kept_lse

    full_lp, kept_lp = lax.map(one_block, (hidden.reshape(count, block_rows, D), sampled.reshape(count, block_rows), keep_bits.reshape(count, block_rows, N_VOCAB)))
    full_lp = full_lp.reshape(TOKENS)
    kept_lp = kept_lp.reshape(TOKENS)
    return full_lp, kept_lp, jnp.mean(kept_lp - full_lp)
```

```python
import jax
import jax.numpy as jnp
from jax import lax
from jax.experimental import pallas as pl
from jax.experimental.pallas import tpu as pltpu
from jax.sharding import PartitionSpec as P

MESH = pl.DeviceIdType.MESH
F32 = jnp.float32

SOFTNESS = 0.7
LOG2E = 1.4426950408889634
EXP_SCALE = LOG2E / SOFTNESS
ABSENT = -2.3819e38

TOKENS = 4096
ROWS = 512
FEAT = 256
CHIP_FEAT = 512
CHIPS = 8
WIDTH = 2432
VBLK = 128
NBLK = 19
TILE = 256
Q = 128
NQ = 4
N_VOCAB = 16
N_ROWS = 8

OWN, UP, DOWN, FAR = (0, 0), (0, 1), (0, 3), (0, 2)
XOWN, XUP, XDOWN, XFAR = (1, 0), (1, 1), (1, 3), (1, 2)

LINKS = {"+": (0, 1), "-": (0, 3), "x": (1, 0)}


def seen_by(chunk, link):
    dx, dy = LINKS[link]
    return ((chunk[0] + dx) % 2, (chunk[1] - dy) % 4)


PROGRAM = [
    ("send", "+", OWN, 0), ("send", "-", OWN, 0), ("send", "x", OWN, 0),
    ("send", "+", OWN, 1), ("send", "-", OWN, 1), ("send", "x", OWN, 1),
    ("send", "+", OWN, 2), ("send", "-", OWN, 2), ("send", "x", OWN, 2),
    ("send", "x", OWN, 3),
    ("own",),
    ("got", UP, 0), ("got", DOWN, 0), ("got", XOWN, 0),
    ("send", "+", DOWN, 0), ("send", "+", OWN, 3),
    ("got", UP, 1), ("got", DOWN, 1), ("got", XOWN, 1),
    ("send", "-", UP, 1), ("send", "-", OWN, 3),
    ("mul", 0, 128, (UP, DOWN, XOWN)),
    ("got", UP, 2), ("got", DOWN, 2), ("got", XOWN, 2),
    ("send", "+", DOWN, 2), ("send", "+", XOWN, 0), ("send", "+", XOWN, 1),
    ("send", "-", XOWN, 0), ("send", "-", XOWN, 1),
    ("mul", 128, 128, (UP, DOWN, XOWN)),
    ("got", FAR, 0), ("got", FAR, 1), ("got", XOWN, 3),
    ("send", "x", FAR, 0), ("send", "x", FAR, 1),
    ("send", "+", XOWN, 2), ("send", "+", XOWN, 3),
    ("mul", 256, 128, (UP, DOWN, XOWN)),
    ("got", UP, 3), ("got", DOWN, 3),
    ("send", "-", UP, 3), ("send", "-", XOWN, 2), ("send", "-", XOWN, 3),
    ("mul", 0, 256, (FAR,)),
    ("got", FAR, 2),
    ("send", "x", FAR, 2),
    ("mul", 384, 128, (UP, DOWN, XOWN)),
    ("got", XUP, 0), ("got", XDOWN, 0), ("got", XFAR, 0),
    ("mul", 0, 128, (XUP, XDOWN, XFAR)),
    ("got", FAR, 3),
    ("send", "x", FAR, 3),
    ("got", XUP, 1), ("got", XDOWN, 1), ("got", XFAR, 1),
    ("finish", 0),
    ("mul", 128, 128, (XUP, XDOWN, XFAR)),
    ("mul", 256, 256, (FAR,)),
    ("got", XUP, 2), ("got", XDOWN, 2), ("got", XFAR, 2),
    ("finish", 1),
    ("mul", 256, 128, (XUP, XDOWN, XFAR)),
    ("got", XUP, 3), ("got", XDOWN, 3), ("got", XFAR, 3),
    ("finish", 2),
    ("mul", 384, 128, (XUP, XDOWN, XFAR)),
    ("finish", 3),
]

SENDS = [step[1:] for step in PROGRAM if step[0] == "send"]
ARRIVALS = {(seen_by(c, link), q): i for i, (link, c, q) in enumerate(SENDS)}
assert len(ARRIVALS) == len(SENDS) == 28

W_ORDER = [OWN, UP, DOWN, XOWN, FAR, XUP, XDOWN, XFAR]


def kernel(
    hidden, weights, sampled, bits,
    full_out, kept_out, mean_out,
    h, w, acc, ids_flat, bits_flat, ids, keeps, top, ktop, total, ktotal, taken,
    stats, gaps,
    load_sem, w_sem, send_sem, recv_sem, share_send, share_recv,
    stat_send, stat_recv, gap_send, gap_recv,
):
    v = lax.axis_index("vocab")
    r = lax.axis_index("rows")
    core = lax.rem(v, 2)
    chip = v // 2
    xh = chip // 4
    y = lax.rem(chip, 4)
    sibling = v + 1 - 2 * core
    mine = pl.ds(pl.multiple_of(core * FEAT, FEAT), FEAT)
    slot = {
        (dx, dy): lax.rem(xh + dx, 2) * 4 + lax.rem(y + dy, 4)
        for dx in range(2)
        for dy in range(4)
    }
    target = {link: slot[d] * 2 + core for link, d in LINKS.items()}

    own_load = pltpu.make_async_copy(hidden, h.at[chip, :, mine], load_sem.at[0])
    own_load.start()
    ids_load = pltpu.make_async_copy(sampled, ids_flat, load_sem.at[1])
    ids_load.start()
    bits_load = pltpu.make_async_copy(bits, bits_flat, load_sem.at[2])
    bits_load.start()
    w_loads = {}
    for i, c in enumerate(W_ORDER):
        rows = pl.ds(pl.multiple_of(slot[c] * CHIP_FEAT, CHIP_FEAT), CHIP_FEAT)
        w_loads[c] = pltpu.make_async_copy(weights.at[rows, :], w.at[slot[c]], w_sem.at[i])
        w_loads[c].start()

    barrier = pltpu.get_barrier_semaphore()
    peers = [lax.rem(v + i, N_VOCAB) for i in range(1, N_VOCAB)]
    row_peers = [lax.rem(r + i, N_ROWS) for i in range(1, N_ROWS)]
    for p in peers:
        pl.semaphore_signal(barrier, inc=1, device_id={"vocab": p}, device_id_type=MESH)
    for p in row_peers:
        pl.semaphore_signal(barrier, inc=1, device_id={"rows": p}, device_id_type=MESH)
    pl.semaphore_wait(barrier, len(peers) + len(row_peers))

    started = []

    def send(i, link, c, q):
        rows = pl.ds(q * Q, Q)
        src = hidden.at[rows, :] if c == OWN else h.at[slot[c], rows, mine]
        copy = pltpu.make_async_remote_copy(
            src_ref=src,
            dst_ref=h.at[slot[c], rows, mine],
            send_sem=send_sem.at[i],
            recv_sem=recv_sem.at[i],
            device_id={"vocab": target[link]},
            device_id_type=MESH,
        )
        copy.start()
        started.append(copy)

    def arrival(i, c, q):
        part = h.at[slot[c], pl.ds(q * Q, Q), mine]
        return pltpu.make_async_remote_copy(
            src_ref=part, dst_ref=part, send_sem=send_sem.at[i], recv_sem=recv_sem.at[i],
            device_id={"vocab": sibling}, device_id_type=MESH,
        )

    def share(i, c, q):
        part = h.at[slot[c], pl.ds(q * Q, Q), mine]
        copy = pltpu.make_async_remote_copy(
            src_ref=part, dst_ref=part, send_sem=share_send.at[i], recv_sem=share_recv.at[i],
            device_id={"vocab": sibling}, device_id_type=MESH,
        )
        copy.start()
        started.append(copy)
        return copy

    shared = {}
    ready_w = set()

    def product(r0, size, chunks, first=False):
        for c in chunks:
            if c not in ready_w:
                w_loads[c].wait()
                ready_w.add(c)
            if c != OWN:
                for q in range(r0 // Q, (r0 + size) // Q):
                    shared[c, q].wait_recv()
        rows = slice(r0, r0 + size)
        for j in range(0, WIDTH, TILE):
            cols = slice(j, min(j + TILE, WIDTH))
            t = None
            for c in chunks:
                d = jnp.dot(h[slot[c], rows, :], w[slot[c], :, cols], preferred_element_type=F32)
                t = d if t is None else t + d
            acc[rows, cols] = t if first else acc[rows, cols] + t

    def finish(q):
        group = 32

        def part(g, _):
            rows = pl.ds(pl.multiple_of(q * Q + g * group, group), group)
            here = pl.ds(pl.multiple_of(g * group, group), group)
            kept_bits = keeps[rows, :]
            token = ids[rows, :] - v * WIDTH - lax.broadcasted_iota(jnp.int32, (group, VBLK), 1)
            m = km = pk = None
            for b in range(NBLK):
                z = acc[rows, b * VBLK:(b + 1) * VBLK]
                kz = jnp.where((kept_bits & (1 << b)) != 0, z, ABSENT)
                hit = jnp.where(token == b * VBLK, z, 0.0)
                m = z if m is None else jnp.maximum(m, z)
                km = kz if km is None else jnp.maximum(km, kz)
                pk = hit if pk is None else pk + hit
            s = jnp.zeros((group, VBLK), F32)
            ks = jnp.zeros((group, VBLK), F32)
            for b in range(NBLK):
                z = acc[rows, b * VBLK:(b + 1) * VBLK]
                kz = jnp.where((kept_bits & (1 << b)) != 0, z, ABSENT)
                s += jnp.exp2((z - m) * EXP_SCALE)
                ks += jnp.exp2((kz - km) * EXP_SCALE)
            top[here, :] = m
            ktop[here, :] = km
            total[here, :] = s
            ktotal[here, :] = ks
            taken[here, :] = pk
            return 0

        lax.fori_loop(0, Q // group, part, 0)

        def combined(maxes, sums):
            mt = maxes[...].T
            st = sums[...].T
            best = jnp.max(mt, axis=0, keepdims=True)
            whole = jnp.sum(st * jnp.exp2((mt - best) * EXP_SCALE), axis=0, keepdims=True)
            return best / SOFTNESS + jnp.log(whole)

        full = combined(top, total)
        kept = combined(ktop, ktotal)
        picked = jnp.sum(taken[...].T, axis=0, keepdims=True) / SOFTNESS
        stats[v, q, 0:1, :] = full
        stats[v, q, 1:2, :] = kept
        stats[v, q, 2:3, :] = picked
        stats[v, q, 3:4, :] = picked
        for i, p in enumerate(peers):
            copy = pltpu.make_async_remote_copy(
                src_ref=stats.at[v, q], dst_ref=stats.at[v, q],
                send_sem=stat_send.at[q, i], recv_sem=stat_recv.at[q, i],
                device_id={"vocab": p}, device_id_type=MESH,
            )
            copy.start()
            started.append(copy)
            stat_copies[q].append(copy)

    def conclude(q):
        for copy in stat_copies[q]:
            copy.wait_recv()
        best = stats[0, q]
        for i in range(1, N_VOCAB):
            best = jnp.maximum(best, stats[i, q])
        whole = jnp.zeros((4, Q), F32)
        chosen = jnp.zeros((4, Q), F32)
        for i in range(N_VOCAB):
            s = stats[i, q]
            whole += jnp.exp(s - best)
            chosen += s
        lse = best + jnp.log(whole)
        picked = chosen[2:3]
        full = picked - lse[0:1]
        kept = picked - lse[1:2]
        full_out[q:q + 1, :] = full
        kept_out[q:q + 1, :] = kept
        return kept - full

    stat_copies = [[] for _ in range(NQ)]

    ids_load.wait()
    bits_load.wait()

    sent = 0
    for step in PROGRAM:
        if step[0] == "send":
            send(sent, *step[1:])
            sent += 1
        elif step[0] == "own":
            own = pltpu.make_async_remote_copy(
                src_ref=hidden, dst_ref=h.at[chip, :, mine],
                send_sem=share_send.at[28], recv_sem=share_recv.at[28],
                device_id={"vocab": sibling}, device_id_type=MESH,
            )
            own.start()
            started.append(own)
            for q in range(NQ):
                rows = slice(q * Q, (q + 1) * Q)
                ids[rows, :] = jnp.broadcast_to(ids_flat[q:q + 1, :], (VBLK, Q)).T
                keeps[rows, :] = jnp.broadcast_to(bits_flat[q:q + 1, :], (VBLK, Q)).T
            own_load.wait()
            own.wait_recv()
            product(0, ROWS, (OWN,), first=True)
        elif step[0] == "got":
            i = ARRIVALS[step[1:]]
            arrival(i, *step[1:]).wait_recv()
            shared[step[1:]] = share(i, *step[1:])
        elif step[0] == "mul":
            product(*step[1:])
        else:
            finish(step[1])

    gap = None
    for q in range(NQ):
        g = conclude(q)
        gap = g if gap is None else gap + g
    gaps[r] = jnp.broadcast_to(gap, (8, Q))
    gap_copies = []
    for i, p in enumerate(row_peers):
        copy = pltpu.make_async_remote_copy(
            src_ref=gaps.at[r], dst_ref=gaps.at[r],
            send_sem=gap_send.at[i], recv_sem=gap_recv.at[i],
            device_id={"rows": p}, device_id_type=MESH,
        )
        copy.start()
        started.append(copy)
        gap_copies.append(copy)
    for copy in started:
        copy.wait_send()
    for copy in gap_copies:
        copy.wait_recv()
    everything = gaps[0]
    for i in range(1, N_ROWS):
        everything += gaps[i]
    mean_out[...] = jnp.sum(everything[0:1], axis=1, keepdims=True) / TOKENS


def per_device(hidden, weights, sampled, keep_bits):
    anywhere = pl.BlockSpec(memory_space=pl.ANY)
    vmem = pl.BlockSpec(memory_space=pltpu.VMEM)
    dma = pltpu.SemaphoreType.DMA
    full, kept, mean = pl.pallas_call(
        kernel,
        out_shape=(
            jax.ShapeDtypeStruct((NQ, Q), F32),
            jax.ShapeDtypeStruct((NQ, Q), F32),
            jax.ShapeDtypeStruct((1, 1), F32),
        ),
        in_specs=[anywhere] * 4,
        out_specs=(vmem, vmem, vmem),
        scratch_shapes=[
            pltpu.VMEM((CHIPS, ROWS, CHIP_FEAT), jnp.bfloat16),
            pltpu.VMEM((CHIPS, CHIP_FEAT, WIDTH), jnp.bfloat16),
            pltpu.VMEM((ROWS, WIDTH), F32),
            pltpu.VMEM((NQ, Q), jnp.int32),
            pltpu.VMEM((NQ, Q), jnp.int32),
            pltpu.VMEM((ROWS, VBLK), jnp.int32),
            pltpu.VMEM((ROWS, VBLK), jnp.int32),
            pltpu.VMEM((Q, VBLK), F32),
            pltpu.VMEM((Q, VBLK), F32),
            pltpu.VMEM((Q, VBLK), F32),
            pltpu.VMEM((Q, VBLK), F32),
            pltpu.VMEM((Q, VBLK), F32),
            pltpu.VMEM((N_VOCAB, NQ, 4, Q), F32),
            pltpu.VMEM((N_ROWS, 8, Q), F32),
            dma((3,)),
            dma((CHIPS,)),
            dma((28,)),
            dma((28,)),
            dma((29,)),
            dma((29,)),
            dma((NQ, N_VOCAB - 1)),
            dma((NQ, N_VOCAB - 1)),
            dma((N_ROWS - 1,)),
            dma((N_ROWS - 1,)),
        ],
        compiler_params=pltpu.CompilerParams(
            collective_id=0, has_side_effects=True, vmem_limit_bytes=56 << 20
        ),
        cost_estimate=pl.CostEstimate(
            flops=2 * ROWS * WIDTH * CHIPS * CHIP_FEAT,
            bytes_accessed=2 * CHIPS * CHIP_FEAT * WIDTH,
            transcendentals=2 * ROWS * WIDTH,
        ),
    )(hidden, weights, sampled.reshape(NQ, Q), keep_bits.reshape(NQ, Q))
    return full.reshape(ROWS), kept.reshape(ROWS), mean.reshape(())


def solution(mesh):
    placed = (P("rows", "vocab"), P(None, "vocab"), P("rows"), P("rows", "vocab"))
    return jax.shard_map(
        per_device,
        mesh=mesh,
        in_specs=placed,
        out_specs=(P("rows"), P("rows"), P()),
        check_vma=False,
    )
```

```python
import jax
import jax.numpy as jnp
from jax import lax
from jax.experimental import pallas as pl
from jax.experimental.pallas import tpu as pltpu
from jax.sharding import PartitionSpec as P

MESH = pl.DeviceIdType.MESH
F32 = jnp.float32

SOFTNESS = 0.7
LOG2E = 1.4426950408889634
EXP_SCALE = LOG2E / SOFTNESS
ABSENT = -2.3819e38

TOKENS = 4096
ROWS = 512
FEAT = 256
CHIP_FEAT = 512
CHIPS = 8
WIDTH = 2432
VBLK = 128
NBLK = 19
TILE = 256
Q = 128
NQ = 4
N_VOCAB = 16
N_ROWS = 8

OWN, UP, DOWN, FAR = (0, 0), (0, 1), (0, 3), (0, 2)
XOWN, XUP, XDOWN, XFAR = (1, 0), (1, 1), (1, 3), (1, 2)

LINKS = {"+": (0, 1), "-": (0, 3), "x": (1, 0)}


def seen_by(chunk, link):
    dx, dy = LINKS[link]
    return ((chunk[0] + dx) % 2, (chunk[1] - dy) % 4)


NEAR = (UP, DOWN, XOWN)
CROSS = (XUP, XDOWN, XFAR)


def at(chunks, r0, n=Q):
    return tuple((c, r0, n) for c in chunks)


PROGRAM = [
    ("send", "+", OWN, 0, 128), ("send", "-", OWN, 256, 128), ("send", "x", OWN, 0, 128),
    ("send", "+", OWN, 128, 128), ("send", "-", OWN, 384, 128), ("send", "x", OWN, 128, 128),
    ("send", "+", OWN, 256, 128), ("send", "-", OWN, 0, 128), ("send", "x", OWN, 256, 128),
    ("send", "x", OWN, 384, 128),
    ("own",),
    ("got", ((DOWN, 0, 128), (UP, 256, 128))),
    ("send", "+", DOWN, 0, 128), ("send", "-", UP, 256, 128),
    ("send", "+", OWN, 384, 128), ("send", "-", OWN, 128, 128),
    ("got", ((XOWN, 0, 128),)),
    ("got", ((DOWN, 128, 128), (UP, 384, 128))),
    ("send", "+", DOWN, 128, 128), ("send", "-", UP, 384, 128),
    ("send", "+", XOWN, 0, 128), ("send", "-", XOWN, 0, 128),
    ("mul", 0, 128, (DOWN, XOWN)),
    ("got", ((XOWN, 128, 128),)),
    ("got", ((DOWN, 256, 128), (UP, 0, 128))),
    ("mul", 128, 128, (DOWN, XOWN)),
    ("mul", 256, 256, (UP,)),
    ("got", ((FAR, 0, 128), (FAR, 256, 128))),
    ("send", "x", FAR, 0, 128), ("send", "x", FAR, 256, 128),
    ("got", ((XOWN, 256, 128), (XOWN, 384, 128))),
    ("send", "+", XOWN, 256, 128), ("send", "-", XOWN, 256, 128),
    ("send", "+", XOWN, 128, 128), ("send", "-", XOWN, 128, 128),
    ("send", "+", XOWN, 384, 128), ("send", "-", XOWN, 384, 128),
    ("mul", 256, 128, (DOWN, XOWN)),
    ("got", ((DOWN, 384, 128), (UP, 128, 128))),
    ("mul", 384, 128, (DOWN, XOWN)),
    ("got", ((FAR, 128, 128), (FAR, 384, 128))),
    ("send", "x", FAR, 128, 128), ("send", "x", FAR, 384, 128),
    ("mul", 0, 256, (UP,)),
    ("got", at(CROSS, 0)),
    ("mul", 0, 512, (FAR,)),
    ("got", at(CROSS, 256)),
    ("last", 0),
    ("got", at(CROSS, 128)),
    ("last", 2),
    ("got", at(CROSS, 384)),
    ("last", 1),
    ("last", 3),
]

SENDS = [step[1:] for step in PROGRAM if step[0] == "send"]
GROUPS = [step[1] for step in PROGRAM if step[0] == "got"]
GROUP_OF = {piece: i for i, group in enumerate(GROUPS) for piece in group}
assert {(seen_by(c, link), r0, n) for link, c, r0, n in SENDS} == set(GROUP_OF)
SENT_ROWS = sum(n for _, _, _, n in SENDS)
assert SENT_ROWS == 7 * ROWS

W_ORDER = [OWN, UP, DOWN, XOWN, FAR, XUP, XDOWN, XFAR]


def kernel(
    hidden, weights, sampled, bits,
    out,
    h, w, acc, kacc, ids_flat, bits_flat, ids, keeps, top, ktop, total, ktotal, taken,
    stats, gaps,
    load_sem, w_sem, send_sem, recv_sem, share_recv,
    stat_send, stat_recv, gap_send, gap_recv,
):
    v = lax.axis_index("vocab")
    r = lax.axis_index("rows")
    core = lax.rem(v, 2)
    chip = v // 2
    xh = chip // 4
    y = lax.rem(chip, 4)
    sibling = v + 1 - 2 * core
    mine = pl.ds(pl.multiple_of(core * FEAT, FEAT), FEAT)
    slot = {
        (dx, dy): lax.rem(xh + dx, 2) * 4 + lax.rem(y + dy, 4)
        for dx in range(2)
        for dy in range(4)
    }
    target = {link: slot[d] * 2 + core for link, d in LINKS.items()}

    own_load = pltpu.make_async_copy(hidden, h.at[chip, :, mine], load_sem.at[0])
    own_load.start()
    ids_load = pltpu.make_async_copy(sampled, ids_flat, load_sem.at[1])
    ids_load.start()
    bits_load = pltpu.make_async_copy(bits, bits_flat, load_sem.at[2])
    bits_load.start()
    w_loads = {}
    for i, c in enumerate(W_ORDER):
        rows = pl.ds(pl.multiple_of(slot[c] * CHIP_FEAT, CHIP_FEAT), CHIP_FEAT)
        w_loads[c] = pltpu.make_async_copy(weights.at[rows, :], w.at[slot[c]], w_sem.at[i])
        if c == OWN:
            w_loads[c].start()

    barrier = pltpu.get_barrier_semaphore()
    peers = [lax.rem(v + i, N_VOCAB) for i in range(1, N_VOCAB)]
    row_peers = [lax.rem(r + i, N_ROWS) for i in range(1, N_ROWS)]
    for p in peers:
        pl.semaphore_signal(barrier, inc=1, device_id={"vocab": p}, device_id_type=MESH)
    for p in row_peers:
        pl.semaphore_signal(barrier, inc=1, device_id={"rows": p}, device_id_type=MESH)
    pl.semaphore_wait(barrier, len(peers) + len(row_peers))

    def send(link, c, r0, n):
        rows = pl.ds(r0, n)
        src = h.at[slot[c], rows, mine]
        pltpu.make_async_remote_copy(
            src_ref=src,
            dst_ref=h.at[slot[c], rows, mine],
            send_sem=send_sem,
            recv_sem=recv_sem.at[GROUP_OF[seen_by(c, link), r0, n]],
            device_id={"vocab": target[link]},
            device_id_type=MESH,
        ).start()

    def wait_rows(n, sem):
        part = h.at[0, pl.ds(0, n), mine]
        pltpu.make_async_copy(part, part, sem).wait()

    def share(src, dst, i):
        pltpu.make_async_remote_copy(
            src_ref=src, dst_ref=dst, send_sem=send_sem, recv_sem=share_recv.at[i],
            device_id={"vocab": sibling}, device_id_type=MESH,
        ).start()

    shared = set()
    ready_w = set()

    def need(group):
        if group not in shared:
            shared.add(group)
            wait_rows(sum(n for _, _, n in GROUPS[group]), share_recv.at[group])

    def product(r0, size, chunks, first=False, seen=None):
        for c in chunks:
            if c not in ready_w:
                w_loads[c].wait()
                ready_w.add(c)
            if c != OWN:
                for (pc, p0, n), group in GROUP_OF.items():
                    if pc == c and p0 < r0 + size and r0 < p0 + n:
                        need(group)
        rows = slice(r0, r0 + size)
        for j in range(0, WIDTH, TILE):
            cols = slice(j, min(j + TILE, WIDTH))
            t = None
            for c in chunks:
                d = jnp.dot(h[slot[c], rows, :], w[slot[c], :, cols], preferred_element_type=F32)
                t = d if t is None else t + d
            t = t if first else acc[rows, cols] + t
            acc[rows, cols] = t
            if seen is not None:
                seen(rows, cols.start, t)

    def finish(q):
        mine_q = slice(q * Q, (q + 1) * Q)
        token = ids[mine_q, :]
        kept_bits = keeps[mine_q, :]

        def seen(rows, c0, t):
            for i in range(t.shape[1] // VBLK):
                b = c0 // VBLK + i
                z = t[:, i * VBLK:(i + 1) * VBLK]
                kz = jnp.where((kept_bits & (1 << b)) != 0, z, ABSENT)
                hit = jnp.where(token == b * VBLK, z, 0.0)
                kacc[:, b * VBLK:(b + 1) * VBLK] = kz
                top[...] = z if b == 0 else jnp.maximum(top[...], z)
                ktop[...] = kz if b == 0 else jnp.maximum(ktop[...], kz)
                taken[...] = hit if b == 0 else taken[...] + hit

        product(q * Q, Q, CROSS, seen=seen)
        group = 32

        def part(g, _):
            rows = pl.ds(pl.multiple_of(q * Q + g * group, group), group)
            here = pl.ds(pl.multiple_of(g * group, group), group)
            m = top[here, :]
            km = ktop[here, :]
            s = jnp.zeros((group, VBLK), F32)
            ks = jnp.zeros((group, VBLK), F32)
            for b in range(NBLK):
                cols = slice(b * VBLK, (b + 1) * VBLK)
                s += jnp.exp2((acc[rows, cols] - m) * EXP_SCALE)
                ks += jnp.exp2((kacc[here, cols] - km) * EXP_SCALE)
            total[here, :] = s
            ktotal[here, :] = ks
            return 0

        lax.fori_loop(0, Q // group, part, 0)

        def combined(maxes, sums):
            mt = maxes[...].T
            st = sums[...].T
            best = jnp.max(mt, axis=0, keepdims=True)
            whole = jnp.sum(st * jnp.exp2((mt - best) * EXP_SCALE), axis=0, keepdims=True)
            return best / SOFTNESS + jnp.log(whole)

        full = combined(top, total)
        kept = combined(ktop, ktotal)
        picked = jnp.sum(taken[...].T, axis=0, keepdims=True) / SOFTNESS
        stats[q, v, 0:1, :] = full
        stats[q, v, 1:2, :] = kept
        stats[q, v, 2:3, :] = picked
        stats[q, v, 3:4, :] = picked
        for p in peers:
            pltpu.make_async_remote_copy(
                src_ref=stats.at[q, v], dst_ref=stats.at[q, v],
                send_sem=stat_send, recv_sem=stat_recv.at[q],
                device_id={"vocab": p}, device_id_type=MESH,
            ).start()

    def conclude(q):
        others = stats.at[q, 0:N_VOCAB - 1]
        pltpu.make_async_copy(others, others, stat_recv.at[q]).wait()
        best = stats[q, 0]
        for i in range(1, N_VOCAB):
            best = jnp.maximum(best, stats[q, i])
        whole = jnp.zeros((4, Q), F32)
        chosen = jnp.zeros((4, Q), F32)
        for i in range(N_VOCAB):
            s = stats[q, i]
            whole += jnp.exp(s - best)
            chosen += s
        lse = best + jnp.log(whole)
        picked = chosen[2:3]
        full = picked - lse[0:1]
        kept = picked - lse[1:2]
        out[q:q + 1, :] = full
        out[NQ + q:NQ + q + 1, :] = kept
        return kept - full

    own_load.wait()
    ids_load.wait()
    bits_load.wait()

    for step in PROGRAM:
        if step[0] == "send":
            send(*step[1:])
        elif step[0] == "own":
            for c in W_ORDER[1:]:
                w_loads[c].start()
            share(h.at[chip, :, mine], h.at[chip, :, mine], len(GROUPS))
            for q in range(NQ):
                rows = slice(q * Q, (q + 1) * Q)
                lanes = lax.broadcasted_iota(jnp.int32, (Q, VBLK), 1) + v * WIDTH
                ids[rows, :] = jnp.broadcast_to(ids_flat[q:q + 1, :], (VBLK, Q)).T - lanes
                keeps[rows, :] = jnp.broadcast_to(bits_flat[q:q + 1, :], (VBLK, Q)).T
            wait_rows(ROWS, share_recv.at[len(GROUPS)])
            product(0, ROWS, (OWN,), first=True)
        elif step[0] == "got":
            group = GROUP_OF[step[1][0]]
            wait_rows(sum(n for _, _, n in step[1]), recv_sem.at[group])
            for c, r0, n in step[1]:
                part = h.at[slot[c], pl.ds(r0, n), mine]
                share(part, part, group)
        elif step[0] == "mul":
            product(*step[1:])
        else:
            finish(step[1])

    gap = None
    for q in range(NQ):
        g = conclude(q)
        gap = g if gap is None else gap + g
    gaps[r] = jnp.broadcast_to(gap, (8, Q))
    for p in row_peers:
        pltpu.make_async_remote_copy(
            src_ref=gaps.at[r], dst_ref=gaps.at[r],
            send_sem=gap_send, recv_sem=gap_recv,
            device_id={"rows": p}, device_id_type=MESH,
        ).start()
    everyone = h.at[:, pl.ds(0, ROWS * 15 // 16), :]
    pltpu.make_async_copy(everyone, everyone, send_sem).wait()
    whole_stats = stats.at[:, 0:N_VOCAB - 1]
    pltpu.make_async_copy(whole_stats, whole_stats, stat_send).wait()
    others = gaps.at[0:N_ROWS - 1]
    pltpu.make_async_copy(others, others, gap_recv).wait()
    everything = gaps[0]
    for i in range(1, N_ROWS):
        everything += gaps[i]
    mean = jnp.sum(everything[0:1], axis=1, keepdims=True) / TOKENS
    out[2 * NQ:2 * NQ + 1, :] = jnp.broadcast_to(mean, (1, Q))
    pltpu.make_async_copy(others, others, gap_send).wait()


def per_device(hidden, weights, sampled, keep_bits):
    anywhere = pl.BlockSpec(memory_space=pl.ANY)
    vmem = pl.BlockSpec(memory_space=pltpu.VMEM)
    dma = pltpu.SemaphoreType.DMA
    out = pl.pallas_call(
        kernel,
        out_shape=jax.ShapeDtypeStruct((2 * NQ + 1, Q), F32),
        in_specs=[anywhere] * 4,
        out_specs=vmem,
        scratch_shapes=[
            pltpu.VMEM((CHIPS, ROWS, CHIP_FEAT), jnp.bfloat16),
            pltpu.VMEM((CHIPS, CHIP_FEAT, WIDTH), jnp.bfloat16),
            pltpu.VMEM((ROWS, WIDTH), F32),
            pltpu.VMEM((Q, WIDTH), F32),
            pltpu.VMEM((NQ, Q), jnp.int32),
            pltpu.VMEM((NQ, Q), jnp.int32),
            pltpu.VMEM((ROWS, VBLK), jnp.int32),
            pltpu.VMEM((ROWS, VBLK), jnp.int32),
            pltpu.VMEM((Q, VBLK), F32),
            pltpu.VMEM((Q, VBLK), F32),
            pltpu.VMEM((Q, VBLK), F32),
            pltpu.VMEM((Q, VBLK), F32),
            pltpu.VMEM((Q, VBLK), F32),
            pltpu.VMEM((NQ, N_VOCAB, 4, Q), F32),
            pltpu.VMEM((N_ROWS, 8, Q), F32),
            dma((3,)),
            dma((CHIPS,)),
            dma,
            dma((len(GROUPS),)),
            dma((len(GROUPS) + 1,)),
            dma,
            dma((NQ,)),
            dma,
            dma,
        ],
        compiler_params=pltpu.CompilerParams(
            collective_id=0, has_side_effects=True, vmem_limit_bytes=56 << 20
        ),
        cost_estimate=pl.CostEstimate(
            flops=2 * ROWS * WIDTH * CHIPS * CHIP_FEAT,
            bytes_accessed=2 * CHIPS * CHIP_FEAT * WIDTH,
            transcendentals=2 * ROWS * WIDTH,
        ),
    )(hidden, weights, sampled.reshape(NQ, Q), keep_bits.reshape(NQ, Q))
    return out[:NQ].reshape(ROWS), out[NQ:2 * NQ].reshape(ROWS), out[2 * NQ, 0]


def solution(mesh):
    placed = (P("rows", "vocab"), P(None, "vocab"), P("rows"), P("rows", "vocab"))
    return jax.shard_map(
        per_device,
        mesh=mesh,
        in_specs=placed,
        out_specs=(P("rows"), P("rows"), P()),
        check_vma=False,
    )
```

```python
import functools

import jax
import jax.numpy as jnp
from jax import lax
from jax.experimental import pallas as pl
from jax.experimental.pallas import tpu as pltpu
from jax.sharding import PartitionSpec as P

MESH = pl.DeviceIdType.MESH
F32 = jnp.float32

SOFTNESS = 0.7
LOG2E = 1.4426950408889634
EXP_SCALE = LOG2E / SOFTNESS
ABSENT = -2.3819e38

TOKENS = 4096
ROWS = 512
FEAT = 256
CHIP_FEAT = 512
CHIPS = 8
WIDTH = 2432
VBLK = 128
NBLK = 19
TILE = 256
Q = 128
NQ = 4
N_VOCAB = 16
N_ROWS = 8

OWN, UP, DOWN, FAR = (0, 0), (0, 1), (0, 3), (0, 2)
XOWN, XUP, XDOWN, XFAR = (1, 0), (1, 1), (1, 3), (1, 2)

LINKS = {"+": (0, 1), "-": (0, 3), "x": (1, 0)}


def seen_by(chunk, link):
    dx, dy = LINKS[link]
    return ((chunk[0] + dx) % 2, (chunk[1] - dy) % 4)


NEAR = (UP, DOWN, XOWN)
CROSS = (XUP, XDOWN, XFAR)


def at(chunks, r0, n=Q):
    return tuple((c, r0, n) for c in chunks)


PROGRAM = [
    ("send", "+", OWN, 0, 128), ("send", "-", OWN, 256, 128), ("send", "x", OWN, 0, 128),
    ("send", "+", OWN, 128, 128), ("send", "-", OWN, 384, 128), ("send", "x", OWN, 128, 128),
    ("send", "+", OWN, 256, 128), ("send", "-", OWN, 0, 128), ("send", "x", OWN, 256, 128),
    ("send", "x", OWN, 384, 128),
    ("own",),
    ("got", ((DOWN, 0, 128), (UP, 256, 128))),
    ("send", "+", DOWN, 0, 128), ("send", "-", UP, 256, 128),
    ("send", "+", OWN, 384, 128), ("send", "-", OWN, 128, 128),
    ("got", ((XOWN, 0, 128),)),
    ("got", ((DOWN, 128, 128), (UP, 384, 128))),
    ("send", "+", DOWN, 128, 128), ("send", "-", UP, 384, 128),
    ("send", "+", XOWN, 0, 128), ("send", "-", XOWN, 0, 128),
    ("mul", 0, 128, (DOWN, XOWN)),
    ("got", ((XOWN, 128, 128),)),
    ("got", ((DOWN, 256, 128), (UP, 0, 128))),
    ("mul", 128, 128, (DOWN, XOWN)),
    ("got", ((FAR, 0, 128), (FAR, 256, 128))),
    ("send", "x", FAR, 0, 128), ("send", "x", FAR, 256, 128),
    ("mul", 256, 256, (UP,)),
    ("got", ((XOWN, 256, 128), (XOWN, 384, 128))),
    ("send", "+", XOWN, 256, 128), ("send", "-", XOWN, 256, 128),
    ("send", "+", XOWN, 128, 128), ("send", "-", XOWN, 128, 128),
    ("send", "+", XOWN, 384, 128), ("send", "-", XOWN, 384, 128),
    ("mul", 256, 128, (DOWN, XOWN)),
    ("got", ((DOWN, 384, 128), (UP, 128, 128))),
    ("got", ((FAR, 128, 128), (FAR, 384, 128))),
    ("send", "x", FAR, 128, 128), ("send", "x", FAR, 384, 128),
    ("mul", 384, 128, (DOWN, XOWN)),
    ("mul", 0, 256, (UP,)),
    ("mul", 0, 256, (FAR,)),
    ("got", at(CROSS, 0)),
    ("mul", 256, 256, (FAR,)),
    ("got", at(CROSS, 256)),
    ("last", 0),
    ("got", at(CROSS, 128)),
    ("last", 2),
    ("got", at(CROSS, 384)),
    ("last", 1),
    ("last", 3),
]

SENDS = [step[1:] for step in PROGRAM if step[0] == "send"]
GROUPS = [step[1] for step in PROGRAM if step[0] == "got"]
GROUP_OF = {piece: i for i, group in enumerate(GROUPS) for piece in group}
assert {(seen_by(c, link), r0, n) for link, c, r0, n in SENDS} == set(GROUP_OF)
SENT_ROWS = sum(n for _, _, _, n in SENDS)
assert SENT_ROWS == 7 * ROWS

W_ORDER = [OWN, UP, DOWN, XOWN, FAR, XUP, XDOWN, XFAR]


def kernel(
    hidden, weights, sampled, bits,
    out,
    h, w, acc, kacc, ids_flat, bits_flat, ids, keeps, top, ktop, total, ktotal, taken,
    stats, gaps,
    load_sem, w_sem, send_sem, recv_sem, share_recv,
    stat_send, stat_recv, gap_send, gap_recv,
):
    v = lax.axis_index("vocab")
    r = lax.axis_index("rows")
    core = lax.rem(v, 2)
    chip = v // 2
    xh = chip // 4
    y = lax.rem(chip, 4)
    sibling = v + 1 - 2 * core
    mine = pl.ds(pl.multiple_of(core * FEAT, FEAT), FEAT)
    slot = {
        (dx, dy): lax.rem(xh + dx, 2) * 4 + lax.rem(y + dy, 4)
        for dx in range(2)
        for dy in range(4)
    }
    target = {link: slot[d] * 2 + core for link, d in LINKS.items()}

    barrier = pltpu.get_barrier_semaphore()
    peers = [lax.rem(v + i, N_VOCAB) for i in range(1, N_VOCAB)]
    row_peers = [lax.rem(r + i, N_ROWS) for i in range(1, N_ROWS)]
    for p in (target["+"], target["-"], target["x"], sibling):
        pl.semaphore_signal(barrier, inc=1, device_id={"vocab": p}, device_id_type=MESH)
    for p in row_peers:
        pl.semaphore_signal(barrier, inc=1, device_id={"rows": p}, device_id_type=MESH)

    own_load = pltpu.make_async_copy(hidden, h.at[chip, :, mine], load_sem.at[0])
    own_load.start()
    ids_load = pltpu.make_async_copy(sampled, ids_flat, load_sem.at[1])
    ids_load.start()
    bits_load = pltpu.make_async_copy(bits, bits_flat, load_sem.at[2])
    bits_load.start()
    w_loads = {}
    for i, c in enumerate(W_ORDER):
        rows = pl.ds(pl.multiple_of(slot[c] * CHIP_FEAT, CHIP_FEAT), CHIP_FEAT)
        w_loads[c] = pltpu.make_async_copy(weights.at[rows, :], w.at[slot[c]], w_sem.at[i])
        if c == OWN:
            w_loads[c].start()

    pl.semaphore_wait(barrier, 4 + len(row_peers))

    def send(link, c, r0, n):
        rows = pl.ds(r0, n)
        src = h.at[slot[c], rows, mine]
        pltpu.make_async_remote_copy(
            src_ref=src,
            dst_ref=h.at[slot[c], rows, mine],
            send_sem=send_sem,
            recv_sem=recv_sem.at[GROUP_OF[seen_by(c, link), r0, n]],
            device_id={"vocab": target[link]},
            device_id_type=MESH,
        ).start()

    def wait_rows(n, sem):
        part = h.at[0, pl.ds(0, n), mine]
        pltpu.make_async_copy(part, part, sem).wait()

    def share(src, dst, i):
        pltpu.make_async_remote_copy(
            src_ref=src, dst_ref=dst, send_sem=send_sem, recv_sem=share_recv.at[i],
            device_id={"vocab": sibling}, device_id_type=MESH,
        ).start()

    shared = set()
    ready_w = set()

    def need(group):
        if group not in shared:
            shared.add(group)
            wait_rows(sum(n for _, _, n in GROUPS[group]), share_recv.at[group])

    def product(r0, size, chunks, first=False, seen=None, beside=()):
        for c in chunks:
            if c not in ready_w:
                w_loads[c].wait()
                ready_w.add(c)
            if c != OWN:
                for (pc, p0, n), group in GROUP_OF.items():
                    if pc == c and p0 < r0 + size and r0 < p0 + n:
                        need(group)
        rows = slice(r0, r0 + size)
        beside = list(beside)
        for j in range(0, WIDTH, TILE):
            cols = slice(j, min(j + TILE, WIDTH))
            t = None
            for c in chunks:
                d = jnp.dot(h[slot[c], rows, :], w[slot[c], :, cols], preferred_element_type=F32)
                t = d if t is None else t + d
            t = t if first else acc[rows, cols] + t
            acc[rows, cols] = t
            if seen is not None:
                seen(rows, cols.start, t)
            if beside:
                beside.pop(0)()
        assert not beside

    def last_product(q, beside):
        mine_q = slice(q * Q, (q + 1) * Q)
        token = ids[mine_q, :]
        kept_bits = keeps[mine_q, :]

        def seen(rows, c0, t):
            for i in range(t.shape[1] // VBLK):
                b = c0 // VBLK + i
                z = t[:, i * VBLK:(i + 1) * VBLK]
                kz = jnp.where((kept_bits & (1 << b)) != 0, z, ABSENT)
                hit = jnp.where(token == b * VBLK, z, 0.0)
                kacc[mine_q, b * VBLK:(b + 1) * VBLK] = kz
                top[mine_q, :] = z if b == 0 else jnp.maximum(top[mine_q, :], z)
                ktop[mine_q, :] = kz if b == 0 else jnp.maximum(ktop[mine_q, :], kz)
                taken[mine_q, :] = hit if b == 0 else taken[mine_q, :] + hit

        product(q * Q, Q, CROSS, seen=seen, beside=beside)

    def sums(q):
        group = 16
        steps = []

        def part(r0):
            rows = slice(r0, r0 + group)
            m = top[rows, :]
            km = ktop[rows, :]
            s = jnp.zeros((group, VBLK), F32)
            ks = jnp.zeros((group, VBLK), F32)
            for b in range(NBLK):
                cols = slice(b * VBLK, (b + 1) * VBLK)
                s += jnp.exp2((acc[rows, cols] - m) * EXP_SCALE)
                ks += jnp.exp2((kacc[rows, cols] - km) * EXP_SCALE)
            total[rows, :] = s
            ktotal[rows, :] = ks

        for r0 in range(q * Q, (q + 1) * Q, group):
            steps.append(functools.partial(part, r0))
        steps.append(functools.partial(combine, q))
        return steps

    def combine(q):
        mine_q = slice(q * Q, (q + 1) * Q)

        def combined(maxes, parts):
            mt = maxes[mine_q, :].T
            st = parts[mine_q, :].T
            best = jnp.max(mt, axis=0, keepdims=True)
            whole = jnp.sum(st * jnp.exp2((mt - best) * EXP_SCALE), axis=0, keepdims=True)
            return best / SOFTNESS + jnp.log(whole)

        full = combined(top, total)
        kept = combined(ktop, ktotal)
        picked = jnp.sum(taken[mine_q, :].T, axis=0, keepdims=True) / SOFTNESS
        stats[v, 0, q:q + 1, :] = full
        stats[v, 1, q:q + 1, :] = kept
        stats[v, 2, q:q + 1, :] = picked

    def lse_of(i):
        best = stats[0, i]
        for d in range(1, N_VOCAB):
            best = jnp.maximum(best, stats[d, i])
        whole = jnp.exp(stats[0, i] - best)
        for d in range(1, N_VOCAB):
            whole += jnp.exp(stats[d, i] - best)
        return best + jnp.log(whole)

    own_load.wait()
    ids_load.wait()
    bits_load.wait()

    pending = []
    for step in PROGRAM:
        if step[0] == "send":
            send(*step[1:])
        elif step[0] == "own":
            for c in W_ORDER[1:]:
                w_loads[c].start()
            share(h.at[chip, :, mine], h.at[chip, :, mine], len(GROUPS))
            for q in range(NQ):
                rows = slice(q * Q, (q + 1) * Q)
                lanes = lax.broadcasted_iota(jnp.int32, (Q, VBLK), 1) + v * WIDTH
                ids[rows, :] = jnp.broadcast_to(ids_flat[q:q + 1, :], (VBLK, Q)).T - lanes
                keeps[rows, :] = jnp.broadcast_to(bits_flat[q:q + 1, :], (VBLK, Q)).T
            wait_rows(ROWS, share_recv.at[len(GROUPS)])
            product(0, ROWS, (OWN,), first=True)
        elif step[0] == "got":
            group = GROUP_OF[step[1][0]]
            wait_rows(sum(n for _, _, n in step[1]), recv_sem.at[group])
            for c, r0, n in step[1]:
                part = h.at[slot[c], pl.ds(r0, n), mine]
                share(part, part, group)
        elif step[0] == "mul":
            product(*step[1:])
        else:
            last_product(step[1], pending)
            pending = sums(step[1])
    for last_step in pending:
        last_step()

    for p in peers:
        pltpu.make_async_remote_copy(
            src_ref=stats.at[v], dst_ref=stats.at[v], send_sem=stat_send, recv_sem=stat_recv,
            device_id={"vocab": p}, device_id_type=MESH,
        ).start()
    others = stats.at[0:N_VOCAB - 1]
    pltpu.make_async_copy(others, others, stat_recv).wait()
    picked = stats[0, 2]
    for d in range(1, N_VOCAB):
        picked += stats[d, 2]
    full = picked - lse_of(0)
    kept = picked - lse_of(1)
    out[0:NQ, :] = full
    out[NQ:2 * NQ, :] = kept
    gap = jnp.sum(kept - full, axis=0, keepdims=True)
    gaps[r] = jnp.broadcast_to(gap, (8, Q))
    for p in row_peers:
        pltpu.make_async_remote_copy(
            src_ref=gaps.at[r], dst_ref=gaps.at[r],
            send_sem=gap_send, recv_sem=gap_recv,
            device_id={"rows": p}, device_id_type=MESH,
        ).start()
    everyone = h.at[:, pl.ds(0, ROWS * 15 // 16), :]
    pltpu.make_async_copy(everyone, everyone, send_sem).wait()
    pltpu.make_async_copy(others, others, stat_send).wait()
    others = gaps.at[0:N_ROWS - 1]
    pltpu.make_async_copy(others, others, gap_recv).wait()
    everything = gaps[0]
    for i in range(1, N_ROWS):
        everything += gaps[i]
    mean = jnp.sum(everything[0:1], axis=1, keepdims=True) / TOKENS
    out[2 * NQ:2 * NQ + 1, :] = jnp.broadcast_to(mean, (1, Q))
    pltpu.make_async_copy(others, others, gap_send).wait()


def per_device(hidden, weights, sampled, keep_bits):
    anywhere = pl.BlockSpec(memory_space=pl.ANY)
    vmem = pl.BlockSpec(memory_space=pltpu.VMEM)
    dma = pltpu.SemaphoreType.DMA
    out = pl.pallas_call(
        kernel,
        out_shape=jax.ShapeDtypeStruct((2 * NQ + 1, Q), F32),
        in_specs=[anywhere] * 4,
        out_specs=vmem,
        scratch_shapes=[
            pltpu.VMEM((CHIPS, ROWS, CHIP_FEAT), jnp.bfloat16),
            pltpu.VMEM((CHIPS, CHIP_FEAT, WIDTH), jnp.bfloat16),
            pltpu.VMEM((ROWS, WIDTH), F32),
            pltpu.VMEM((ROWS, WIDTH), F32),
            pltpu.VMEM((NQ, Q), jnp.int32),
            pltpu.VMEM((NQ, Q), jnp.int32),
            pltpu.VMEM((ROWS, VBLK), jnp.int32),
            pltpu.VMEM((ROWS, VBLK), jnp.int32),
            pltpu.VMEM((ROWS, VBLK), F32),
            pltpu.VMEM((ROWS, VBLK), F32),
            pltpu.VMEM((ROWS, VBLK), F32),
            pltpu.VMEM((ROWS, VBLK), F32),
            pltpu.VMEM((ROWS, VBLK), F32),
            pltpu.VMEM((N_VOCAB, 3, NQ, Q), F32),
            pltpu.VMEM((N_ROWS, 8, Q), F32),
            dma((3,)),
            dma((CHIPS,)),
            dma,
            dma((len(GROUPS),)),
            dma((len(GROUPS) + 1,)),
            dma,
            dma,
            dma,
            dma,
        ],
        compiler_params=pltpu.CompilerParams(
            collective_id=0, has_side_effects=True, vmem_limit_bytes=56 << 20
        ),
        cost_estimate=pl.CostEstimate(
            flops=2 * ROWS * WIDTH * CHIPS * CHIP_FEAT,
            bytes_accessed=2 * CHIPS * CHIP_FEAT * WIDTH,
            transcendentals=2 * ROWS * WIDTH,
        ),
    )(hidden, weights, sampled.reshape(NQ, Q), keep_bits.reshape(NQ, Q))
    return out[:NQ].reshape(ROWS), out[NQ:2 * NQ].reshape(ROWS), out[2 * NQ, 0]


def solution(mesh):
    placed = (P("rows", "vocab"), P(None, "vocab"), P("rows"), P("rows", "vocab"))
    return jax.shard_map(
        per_device,
        mesh=mesh,
        in_specs=placed,
        out_specs=(P("rows"), P("rows"), P()),
        check_vma=False,
    )
```

```python
import functools

import jax
import jax.numpy as jnp
from jax import lax
from jax.experimental import pallas as pl
from jax.experimental.pallas import tpu as pltpu
from jax.sharding import PartitionSpec as P

MESH = pl.DeviceIdType.MESH
F32 = jnp.float32

SOFTNESS = 0.7
LOG2E = 1.4426950408889634
EXP_SCALE = LOG2E / SOFTNESS
ABSENT = -2.3819e38

TOKENS = 4096
ROWS = 512
FEAT = 256
CHIP_FEAT = 512
CHIPS = 8
WIDTH = 2432
VBLK = 128
NBLK = 19
TILE = 256
Q = 128
NQ = 4
N_VOCAB = 16
N_ROWS = 8

OWN, UP, DOWN, FAR = (0, 0), (0, 1), (0, 3), (0, 2)
XOWN, XUP, XDOWN, XFAR = (1, 0), (1, 1), (1, 3), (1, 2)

LINKS = {"+": (0, 1), "-": (0, 3), "x": (1, 0)}


def seen_by(chunk, link):
    dx, dy = LINKS[link]
    return ((chunk[0] + dx) % 2, (chunk[1] - dy) % 4)


NEAR = (UP, DOWN, XOWN)
CROSS = (XUP, XDOWN, XFAR)


def at(chunks, r0, n=Q):
    return tuple((c, r0, n) for c in chunks)


PROGRAM = [
    ("send", "+", OWN, 0, 128), ("send", "-", OWN, 256, 128), ("send", "x", OWN, 0, 128),
    ("send", "+", OWN, 128, 128), ("send", "-", OWN, 384, 128), ("send", "x", OWN, 128, 128),
    ("send", "+", OWN, 256, 128), ("send", "-", OWN, 0, 128), ("send", "x", OWN, 256, 128),
    ("send", "x", OWN, 384, 128),
    ("own",),
    ("got", ((DOWN, 0, 128), (UP, 256, 128))),
    ("send", "+", DOWN, 0, 128), ("send", "-", UP, 256, 128),
    ("send", "+", OWN, 384, 128), ("send", "-", OWN, 128, 128),
    ("got", ((XOWN, 0, 128),)),
    ("mul", 0, 128, (DOWN,)),
    ("mul", 256, 128, (UP,)),
    ("got", ((DOWN, 128, 128), (UP, 384, 128))),
    ("send", "+", DOWN, 128, 128), ("send", "-", UP, 384, 128),
    ("send", "+", XOWN, 0, 128), ("send", "-", XOWN, 0, 128),
    ("got", ((XOWN, 128, 128),)),
    ("mul", 128, 128, (DOWN,)),
    ("mul", 384, 128, (UP,)),
    ("got", ((DOWN, 256, 128), (UP, 0, 128))),
    ("got", ((FAR, 0, 128), (FAR, 256, 128))),
    ("send", "x", FAR, 0, 128), ("send", "x", FAR, 256, 128),
    ("mul", 0, 128, (UP, XOWN)),
    ("got", ((XOWN, 256, 128), (XOWN, 384, 128))),
    ("send", "+", XOWN, 256, 128), ("send", "-", XOWN, 256, 128),
    ("send", "+", XOWN, 128, 128), ("send", "-", XOWN, 128, 128),
    ("send", "+", XOWN, 384, 128), ("send", "-", XOWN, 384, 128),
    ("got", ((DOWN, 384, 128), (UP, 128, 128))),
    ("mul", 256, 128, (DOWN, XOWN)),
    ("got", ((FAR, 128, 128), (FAR, 384, 128))),
    ("send", "x", FAR, 128, 128), ("send", "x", FAR, 384, 128),
    ("mul", 128, 128, (UP, XOWN)),
    ("mul", 384, 128, (DOWN, XOWN)),
    ("mul", 0, 256, (FAR,)),
    ("got", at(CROSS, 0)),
    ("mul", 256, 256, (FAR,)),
    ("got", at(CROSS, 256)),
    ("last", 0),
    ("got", at(CROSS, 128)),
    ("last", 2),
    ("got", at(CROSS, 384)),
    ("last", 1),
    ("last", 3),
]

SENDS = [step[1:] for step in PROGRAM if step[0] == "send"]
GROUPS = [step[1] for step in PROGRAM if step[0] == "got"]
GROUP_OF = {piece: i for i, group in enumerate(GROUPS) for piece in group}
assert {(seen_by(c, link), r0, n) for link, c, r0, n in SENDS} == set(GROUP_OF)
SENT_ROWS = sum(n for _, _, _, n in SENDS)
assert SENT_ROWS == 7 * ROWS

W_ORDER = [OWN, UP, DOWN, XOWN, FAR, XUP, XDOWN, XFAR]


def kernel(
    hidden, weights, sampled, bits,
    out,
    h, w, acc, kacc, ids_flat, bits_flat, ids, keeps, top, ktop, total, ktotal, taken,
    stats, gaps,
    load_sem, w_sem, send_sem, recv_sem, share_recv,
    stat_send, stat_recv, gap_send, gap_recv,
):
    v = lax.axis_index("vocab")
    r = lax.axis_index("rows")
    core = lax.rem(v, 2)
    chip = v // 2
    xh = chip // 4
    y = lax.rem(chip, 4)
    sibling = v + 1 - 2 * core
    mine = pl.ds(pl.multiple_of(core * FEAT, FEAT), FEAT)
    slot = {
        (dx, dy): lax.rem(xh + dx, 2) * 4 + lax.rem(y + dy, 4)
        for dx in range(2)
        for dy in range(4)
    }
    target = {link: slot[d] * 2 + core for link, d in LINKS.items()}

    barrier = pltpu.get_barrier_semaphore()
    peers = [lax.rem(v + i, N_VOCAB) for i in range(1, N_VOCAB)]
    row_peers = [lax.rem(r + i, N_ROWS) for i in range(1, N_ROWS)]
    for p in (target["+"], target["-"], target["x"], sibling):
        pl.semaphore_signal(barrier, inc=1, device_id={"vocab": p}, device_id_type=MESH)
    for p in row_peers:
        pl.semaphore_signal(barrier, inc=1, device_id={"rows": p}, device_id_type=MESH)

    own_load = pltpu.make_async_copy(hidden, h.at[chip, :, mine], load_sem.at[0])
    own_load.start()
    ids_load = pltpu.make_async_copy(sampled, ids_flat, load_sem.at[1])
    ids_load.start()
    bits_load = pltpu.make_async_copy(bits, bits_flat, load_sem.at[2])
    bits_load.start()
    w_loads = {}
    for i, c in enumerate(W_ORDER):
        rows = pl.ds(pl.multiple_of(slot[c] * CHIP_FEAT, CHIP_FEAT), CHIP_FEAT)
        w_loads[c] = pltpu.make_async_copy(weights.at[rows, :], w.at[slot[c]], w_sem.at[i])
        if c == OWN:
            w_loads[c].start()

    pl.semaphore_wait(barrier, 4 + len(row_peers))

    def send(link, c, r0, n):
        rows = pl.ds(r0, n)
        src = h.at[slot[c], rows, mine]
        pltpu.make_async_remote_copy(
            src_ref=src,
            dst_ref=h.at[slot[c], rows, mine],
            send_sem=send_sem,
            recv_sem=recv_sem.at[GROUP_OF[seen_by(c, link), r0, n]],
            device_id={"vocab": target[link]},
            device_id_type=MESH,
        ).start()

    def wait_rows(n, sem):
        part = h.at[0, pl.ds(0, n), mine]
        pltpu.make_async_copy(part, part, sem).wait()

    def share(src, dst, i):
        pltpu.make_async_remote_copy(
            src_ref=src, dst_ref=dst, send_sem=send_sem, recv_sem=share_recv.at[i],
            device_id={"vocab": sibling}, device_id_type=MESH,
        ).start()

    shared = set()
    ready_w = set()

    def need(group):
        if group not in shared:
            shared.add(group)
            wait_rows(sum(n for _, _, n in GROUPS[group]), share_recv.at[group])

    def product(r0, size, chunks, first=False, seen=None, beside=()):
        for c in chunks:
            if c not in ready_w:
                w_loads[c].wait()
                ready_w.add(c)
            if c != OWN:
                for (pc, p0, n), group in GROUP_OF.items():
                    if pc == c and p0 < r0 + size and r0 < p0 + n:
                        need(group)
        rows = slice(r0, r0 + size)
        beside = list(beside)
        for j in range(0, WIDTH, TILE):
            cols = slice(j, min(j + TILE, WIDTH))
            t = None
            for c in chunks:
                d = jnp.dot(h[slot[c], rows, :], w[slot[c], :, cols], preferred_element_type=F32)
                t = d if t is None else t + d
            t = t if first else acc[rows, cols] + t
            acc[rows, cols] = t
            if seen is not None:
                seen(rows, cols.start, t)
            if beside:
                beside.pop(0)()
        assert not beside

    def last_product(q, beside):
        mine_q = slice(q * Q, (q + 1) * Q)
        token = ids[mine_q, :]
        kept_bits = keeps[mine_q, :]

        def seen(rows, c0, t):
            for i in range(t.shape[1] // VBLK):
                b = c0 // VBLK + i
                z = t[:, i * VBLK:(i + 1) * VBLK]
                kz = jnp.where((kept_bits & (1 << b)) != 0, z, ABSENT)
                hit = jnp.where(token == b * VBLK, z, 0.0)
                kacc[mine_q, b * VBLK:(b + 1) * VBLK] = kz
                top[mine_q, :] = z if b == 0 else jnp.maximum(top[mine_q, :], z)
                ktop[mine_q, :] = kz if b == 0 else jnp.maximum(ktop[mine_q, :], kz)
                taken[mine_q, :] = hit if b == 0 else taken[mine_q, :] + hit

        product(q * Q, Q, CROSS, seen=seen, beside=beside)

    def sums(q):
        group = 16
        steps = []

        def part(r0):
            rows = slice(r0, r0 + group)
            m = top[rows, :]
            km = ktop[rows, :]
            s = jnp.zeros((group, VBLK), F32)
            ks = jnp.zeros((group, VBLK), F32)
            for b in range(NBLK):
                cols = slice(b * VBLK, (b + 1) * VBLK)
                s += jnp.exp2((acc[rows, cols] - m) * EXP_SCALE)
                ks += jnp.exp2((kacc[rows, cols] - km) * EXP_SCALE)
            total[rows, :] = s
            ktotal[rows, :] = ks

        for r0 in range(q * Q, (q + 1) * Q, group):
            steps.append(functools.partial(part, r0))
        steps.append(functools.partial(combine, q))
        return steps

    def combine(q):
        mine_q = slice(q * Q, (q + 1) * Q)

        def combined(maxes, parts):
            mt = maxes[mine_q, :].T
            st = parts[mine_q, :].T
            best = jnp.max(mt, axis=0, keepdims=True)
            whole = jnp.sum(st * jnp.exp2((mt - best) * EXP_SCALE), axis=0, keepdims=True)
            return best / SOFTNESS + jnp.log(whole)

        full = combined(top, total)
        kept = combined(ktop, ktotal)
        picked = jnp.sum(taken[mine_q, :].T, axis=0, keepdims=True) / SOFTNESS
        stats[v, 0, q:q + 1, :] = full
        stats[v, 1, q:q + 1, :] = kept
        stats[v, 2, q:q + 1, :] = picked

    def lse_of(i):
        best = stats[0, i]
        for d in range(1, N_VOCAB):
            best = jnp.maximum(best, stats[d, i])
        whole = jnp.exp(stats[0, i] - best)
        for d in range(1, N_VOCAB):
            whole += jnp.exp(stats[d, i] - best)
        return best + jnp.log(whole)

    own_load.wait()
    ids_load.wait()
    bits_load.wait()

    pending = []
    for step in PROGRAM:
        if step[0] == "send":
            send(*step[1:])
        elif step[0] == "own":
            for c in W_ORDER[1:]:
                w_loads[c].start()
            share(h.at[chip, :, mine], h.at[chip, :, mine], len(GROUPS))
            for q in range(NQ):
                rows = slice(q * Q, (q + 1) * Q)
                lanes = lax.broadcasted_iota(jnp.int32, (Q, VBLK), 1) + v * WIDTH
                ids[rows, :] = jnp.broadcast_to(ids_flat[q:q + 1, :], (VBLK, Q)).T - lanes
                keeps[rows, :] = jnp.broadcast_to(bits_flat[q:q + 1, :], (VBLK, Q)).T
            wait_rows(ROWS, share_recv.at[len(GROUPS)])
            product(0, ROWS, (OWN,), first=True)
        elif step[0] == "got":
            group = GROUP_OF[step[1][0]]
            wait_rows(sum(n for _, _, n in step[1]), recv_sem.at[group])
            for c, r0, n in step[1]:
                part = h.at[slot[c], pl.ds(r0, n), mine]
                share(part, part, group)
        elif step[0] == "mul":
            product(*step[1:])
        else:
            last_product(step[1], pending)
            pending = sums(step[1])
    for last_step in pending:
        last_step()

    for p in peers:
        pltpu.make_async_remote_copy(
            src_ref=stats.at[v], dst_ref=stats.at[v], send_sem=stat_send, recv_sem=stat_recv,
            device_id={"vocab": p}, device_id_type=MESH,
        ).start()
    others = stats.at[0:N_VOCAB - 1]
    pltpu.make_async_copy(others, others, stat_recv).wait()
    picked = stats[0, 2]
    for d in range(1, N_VOCAB):
        picked += stats[d, 2]
    full = picked - lse_of(0)
    kept = picked - lse_of(1)
    out[0:NQ, :] = full
    out[NQ:2 * NQ, :] = kept
    gap = jnp.sum(kept - full, axis=0, keepdims=True)
    gaps[r] = jnp.broadcast_to(gap, (8, Q))
    for p in row_peers:
        pltpu.make_async_remote_copy(
            src_ref=gaps.at[r], dst_ref=gaps.at[r],
            send_sem=gap_send, recv_sem=gap_recv,
            device_id={"rows": p}, device_id_type=MESH,
        ).start()
    everyone = h.at[:, pl.ds(0, ROWS * 15 // 16), :]
    pltpu.make_async_copy(everyone, everyone, send_sem).wait()
    pltpu.make_async_copy(others, others, stat_send).wait()
    others = gaps.at[0:N_ROWS - 1]
    pltpu.make_async_copy(others, others, gap_recv).wait()
    everything = gaps[0]
    for i in range(1, N_ROWS):
        everything += gaps[i]
    lane = lax.broadcasted_iota(jnp.int32, (NQ, Q), 0)
    out[2 * NQ:, :] = jnp.where(lane == 0, everything[0:NQ] / TOKENS, 0.0)
    pltpu.make_async_copy(others, others, gap_send).wait()


def per_device(hidden, weights, sampled, keep_bits):
    anywhere = pl.BlockSpec(memory_space=pl.ANY)
    vmem = pl.BlockSpec(memory_space=pltpu.VMEM)
    dma = pltpu.SemaphoreType.DMA
    out = pl.pallas_call(
        kernel,
        out_shape=jax.ShapeDtypeStruct((3 * NQ, Q), F32),
        in_specs=[anywhere] * 4,
        out_specs=vmem,
        scratch_shapes=[
            pltpu.VMEM((CHIPS, ROWS, CHIP_FEAT), jnp.bfloat16),
            pltpu.VMEM((CHIPS, CHIP_FEAT, WIDTH), jnp.bfloat16),
            pltpu.VMEM((ROWS, WIDTH), F32),
            pltpu.VMEM((ROWS, WIDTH), F32),
            pltpu.VMEM((NQ, Q), jnp.int32),
            pltpu.VMEM((NQ, Q), jnp.int32),
            pltpu.VMEM((ROWS, VBLK), jnp.int32),
            pltpu.VMEM((ROWS, VBLK), jnp.int32),
            pltpu.VMEM((ROWS, VBLK), F32),
            pltpu.VMEM((ROWS, VBLK), F32),
            pltpu.VMEM((ROWS, VBLK), F32),
            pltpu.VMEM((ROWS, VBLK), F32),
            pltpu.VMEM((ROWS, VBLK), F32),
            pltpu.VMEM((N_VOCAB, 3, NQ, Q), F32),
            pltpu.VMEM((N_ROWS, 8, Q), F32),
            dma((3,)),
            dma((CHIPS,)),
            dma,
            dma((len(GROUPS),)),
            dma((len(GROUPS) + 1,)),
            dma,
            dma,
            dma,
            dma,
        ],
        compiler_params=pltpu.CompilerParams(
            collective_id=0, has_side_effects=True, vmem_limit_bytes=56 << 20
        ),
        cost_estimate=pl.CostEstimate(
            flops=2 * ROWS * WIDTH * CHIPS * CHIP_FEAT,
            bytes_accessed=2 * CHIPS * CHIP_FEAT * WIDTH,
            transcendentals=2 * ROWS * WIDTH,
        ),
    )(hidden, weights, sampled.reshape(NQ, Q), keep_bits.reshape(NQ, Q))
    out = out.reshape(3, ROWS)
    return out[0], out[1], jnp.sum(out[2])


def solution(mesh):
    placed = (P("rows", "vocab"), P(None, "vocab"), P("rows"), P("rows", "vocab"))
    return jax.shard_map(
        per_device,
        mesh=mesh,
        in_specs=placed,
        out_specs=(P("rows"), P("rows"), P()),
        check_vma=False,
    )
```

```python
import functools

import jax
import jax.numpy as jnp
from jax import lax
from jax.experimental import pallas as pl
from jax.experimental.pallas import tpu as pltpu
from jax.sharding import PartitionSpec as P

MESH = pl.DeviceIdType.MESH
F32 = jnp.float32

SOFTNESS = 0.7
LOG2E = 1.4426950408889634
EXP_SCALE = LOG2E / SOFTNESS
ABSENT = -2.3819e38

TOKENS = 4096
ROWS = 512
FEAT = 256
CHIP_FEAT = 512
CHIPS = 8
WIDTH = 2432
VBLK = 128
NBLK = 19
TILE = 256
Q = 128
NQ = 4
N_VOCAB = 16
N_ROWS = 8

OWN, UP, DOWN, FAR = (0, 0), (0, 1), (0, 3), (0, 2)
XOWN, XUP, XDOWN, XFAR = (1, 0), (1, 1), (1, 3), (1, 2)

LINKS = {"+": (0, 1), "-": (0, 3), "x": (1, 0)}


def seen_by(chunk, link):
    dx, dy = LINKS[link]
    return ((chunk[0] + dx) % 2, (chunk[1] - dy) % 4)


NEAR = (UP, DOWN, XOWN)
CROSS = (XUP, XDOWN, XFAR)


def at(chunks, r0, n=Q):
    return tuple((c, r0, n) for c in chunks)


PROGRAM = [
    ("send", "+", OWN, 0, 128), ("send", "-", OWN, 256, 128), ("send", "x", OWN, 0, 128),
    ("send", "+", OWN, 128, 128), ("send", "-", OWN, 384, 128), ("send", "x", OWN, 128, 128),
    ("send", "+", OWN, 256, 128), ("send", "-", OWN, 0, 128), ("send", "x", OWN, 256, 128),
    ("send", "x", OWN, 384, 128),
    ("own",),
    ("got", ((DOWN, 0, 128), (UP, 256, 128))),
    ("send", "+", DOWN, 0, 128), ("send", "-", UP, 256, 128),
    ("send", "+", OWN, 384, 128), ("send", "-", OWN, 128, 128),
    ("got", ((XOWN, 0, 128),)),
    ("mul", 0, 128, (DOWN,)),
    ("mul", 256, 128, (UP,)),
    ("got", ((DOWN, 128, 128), (UP, 384, 128))),
    ("send", "+", DOWN, 128, 128), ("send", "-", UP, 384, 128),
    ("send", "+", XOWN, 0, 128), ("send", "-", XOWN, 0, 128),
    ("got", ((XOWN, 128, 128),)),
    ("mul", 128, 128, (DOWN,)),
    ("mul", 384, 128, (UP,)),
    ("got", ((DOWN, 256, 128), (UP, 0, 128))),
    ("got", ((FAR, 0, 128), (FAR, 256, 128))),
    ("send", "x", FAR, 0, 128), ("send", "x", FAR, 256, 128),
    ("mul", 0, 128, (UP, XOWN)),
    ("got", ((XOWN, 256, 128), (XOWN, 384, 128))),
    ("send", "+", XOWN, 256, 128), ("send", "-", XOWN, 256, 128),
    ("send", "+", XOWN, 128, 128), ("send", "-", XOWN, 128, 128),
    ("send", "+", XOWN, 384, 128), ("send", "-", XOWN, 384, 128),
    ("got", ((DOWN, 384, 128), (UP, 128, 128))),
    ("mul", 256, 128, (DOWN, XOWN)),
    ("got", ((FAR, 128, 128), (FAR, 384, 128))),
    ("send", "x", FAR, 128, 128), ("send", "x", FAR, 384, 128),
    ("mul", 128, 128, (UP, XOWN)),
    ("mul", 384, 128, (DOWN, XOWN)),
    ("mul", 0, 256, (FAR,)),
    ("got", at(CROSS, 0)),
    ("mul", 256, 256, (FAR,)),
    ("got", at(CROSS, 256)),
    ("last", 0),
    ("got", at(CROSS, 128)),
    ("last", 2),
    ("got", at(CROSS, 384)),
    ("last", 1),
    ("last", 3),
]

SENDS = [step[1:] for step in PROGRAM if step[0] == "send"]
GROUPS = [step[1] for step in PROGRAM if step[0] == "got"]
GROUP_OF = {piece: i for i, group in enumerate(GROUPS) for piece in group}
assert {(seen_by(c, link), r0, n) for link, c, r0, n in SENDS} == set(GROUP_OF)
SENT_ROWS = sum(n for _, _, _, n in SENDS)
assert SENT_ROWS == 7 * ROWS

W_ORDER = [OWN, UP, DOWN, XOWN, FAR, XUP, XDOWN, XFAR]


def kernel(
    hidden, weights, sampled, bits,
    out,
    h, w, acc, ids_flat, bits_flat, ids, keeps, top, ktop, total, ktotal, taken,
    stats, gaps,
    load_sem, w_sem, send_sem, recv_sem, share_recv,
    stat_send, stat_recv, gap_send, gap_recv,
):
    v = lax.axis_index("vocab")
    r = lax.axis_index("rows")
    core = lax.rem(v, 2)
    chip = v // 2
    xh = chip // 4
    y = lax.rem(chip, 4)
    sibling = v + 1 - 2 * core
    mine = pl.ds(pl.multiple_of(core * FEAT, FEAT), FEAT)
    slot = {
        (dx, dy): lax.rem(xh + dx, 2) * 4 + lax.rem(y + dy, 4)
        for dx in range(2)
        for dy in range(4)
    }
    target = {link: slot[d] * 2 + core for link, d in LINKS.items()}

    barrier = pltpu.get_barrier_semaphore()
    hops = (0, 1, 2, 1)
    places = [(dx, dy, dk) for dx in range(2) for dy in range(4) for dk in range(2)]
    places.sort(key=lambda place: -2 * place[0] - hops[place[1]])
    peers = [
        slot[dx, dy] * 2 + lax.rem(core + dk, 2)
        for dx, dy, dk in places
        if (dx, dy, dk) != (0, 0, 0)
    ]
    row_places = [(dz, dx) for dz in range(4) for dx in range(2) if (dz, dx) != (0, 0)]
    row_places.sort(key=lambda place: -hops[place[0]] - place[1])
    row_peers = [
        lax.rem(r // 2 + dz, 4) * 2 + lax.rem(lax.rem(r, 2) + dx, 2) for dz, dx in row_places
    ]
    for p in (target["+"], target["-"], target["x"], sibling):
        pl.semaphore_signal(barrier, inc=1, device_id={"vocab": p}, device_id_type=MESH)
    for p in row_peers:
        pl.semaphore_signal(barrier, inc=1, device_id={"rows": p}, device_id_type=MESH)

    own_load = pltpu.make_async_copy(hidden, h.at[chip, :, mine], load_sem.at[0])
    own_load.start()
    ids_load = pltpu.make_async_copy(sampled, ids_flat, load_sem.at[1])
    ids_load.start()
    bits_load = pltpu.make_async_copy(bits, bits_flat, load_sem.at[2])
    bits_load.start()
    w_loads = {}
    for i, c in enumerate(W_ORDER):
        rows = pl.ds(pl.multiple_of(slot[c] * CHIP_FEAT, CHIP_FEAT), CHIP_FEAT)
        w_loads[c] = pltpu.make_async_copy(weights.at[rows, :], w.at[slot[c]], w_sem.at[i])
        if c == OWN:
            w_loads[c].start()

    pl.semaphore_wait(barrier, 4 + len(row_peers))

    def send(link, c, r0, n):
        rows = pl.ds(r0, n)
        src = h.at[slot[c], rows, mine]
        pltpu.make_async_remote_copy(
            src_ref=src,
            dst_ref=h.at[slot[c], rows, mine],
            send_sem=send_sem,
            recv_sem=recv_sem.at[GROUP_OF[seen_by(c, link), r0, n]],
            device_id={"vocab": target[link]},
            device_id_type=MESH,
        ).start()

    def wait_rows(n, sem):
        part = h.at[0, pl.ds(0, n), mine]
        pltpu.make_async_copy(part, part, sem).wait()

    def share(src, dst, i):
        pltpu.make_async_remote_copy(
            src_ref=src, dst_ref=dst, send_sem=send_sem, recv_sem=share_recv.at[i],
            device_id={"vocab": sibling}, device_id_type=MESH,
        ).start()

    shared = set()
    ready_w = set()

    def need(group):
        if group not in shared:
            shared.add(group)
            wait_rows(sum(n for _, _, n in GROUPS[group]), share_recv.at[group])

    def product(r0, size, chunks, first=False, seen=None, beside=()):
        for c in chunks:
            if c not in ready_w:
                w_loads[c].wait()
                ready_w.add(c)
            if c != OWN:
                for (pc, p0, n), group in GROUP_OF.items():
                    if pc == c and p0 < r0 + size and r0 < p0 + n:
                        need(group)
        rows = slice(r0, r0 + size)
        beside = list(beside)
        for j in range(0, WIDTH, TILE):
            cols = slice(j, min(j + TILE, WIDTH))
            t = None
            for c in chunks:
                d = jnp.dot(h[slot[c], rows, :], w[slot[c], :, cols], preferred_element_type=F32)
                t = d if t is None else t + d
            t = t if first else acc[rows, cols] + t
            acc[rows, cols] = t
            if seen is not None:
                seen(rows, cols.start, t)
            if beside:
                beside.pop(0)()
        assert not beside

    def last_product(q, beside):
        mine_q = slice(q * Q, (q + 1) * Q)
        token = ids[mine_q, :]
        kept_bits = keeps[mine_q, :]

        def seen(rows, c0, t):
            for i in range(t.shape[1] // VBLK):
                b = c0 // VBLK + i
                z = t[:, i * VBLK:(i + 1) * VBLK]
                kz = jnp.where((kept_bits & (1 << b)) != 0, z, ABSENT)
                hit = jnp.where(token == b * VBLK, z, 0.0)
                top[mine_q, :] = z if b == 0 else jnp.maximum(top[mine_q, :], z)
                ktop[mine_q, :] = kz if b == 0 else jnp.maximum(ktop[mine_q, :], kz)
                taken[mine_q, :] = hit if b == 0 else taken[mine_q, :] + hit

        product(q * Q, Q, CROSS, seen=seen, beside=beside)

    def sums(q):
        group = 16
        steps = []

        def part(r0):
            rows = slice(r0, r0 + group)
            m = top[rows, :]
            km = ktop[rows, :]
            s = jnp.zeros((group, VBLK), F32)
            ks = jnp.zeros((group, VBLK), F32)
            for b in range(NBLK):
                cols = slice(b * VBLK, (b + 1) * VBLK)
                s += jnp.exp2((acc[rows, cols] - m) * EXP_SCALE)
                kz = jnp.where((keeps[rows, :] & (1 << b)) != 0, acc[rows, cols], ABSENT)
                ks += jnp.exp2((kz - km) * EXP_SCALE)
            total[rows, :] = s
            ktotal[rows, :] = ks

        for r0 in range(q * Q, (q + 1) * Q, group):
            steps.append(functools.partial(part, r0))
        steps.append(functools.partial(combine, q))
        return steps

    def combine(q):
        mine_q = slice(q * Q, (q + 1) * Q)

        def combined(maxes, parts):
            mt = maxes[mine_q, :].T
            st = parts[mine_q, :].T
            best = jnp.max(mt, axis=0, keepdims=True)
            whole = jnp.sum(st * jnp.exp2((mt - best) * EXP_SCALE), axis=0, keepdims=True)
            return best / SOFTNESS + jnp.log(whole)

        full = combined(top, total)
        kept = combined(ktop, ktotal)
        picked = jnp.sum(taken[mine_q, :].T, axis=0, keepdims=True) / SOFTNESS
        stats[v, 0, q:q + 1, :] = full
        stats[v, 1, q:q + 1, :] = kept
        stats[v, 2, q:q + 1, :] = picked

    def lse_of(i):
        best = stats[0, i]
        for d in range(1, N_VOCAB):
            best = jnp.maximum(best, stats[d, i])
        whole = jnp.exp(stats[0, i] - best)
        for d in range(1, N_VOCAB):
            whole += jnp.exp(stats[d, i] - best)
        return best + jnp.log(whole)

    own_load.wait()
    ids_load.wait()
    bits_load.wait()

    pending = []
    for step in PROGRAM:
        if step[0] == "send":
            send(*step[1:])
        elif step[0] == "own":
            for c in W_ORDER[1:]:
                w_loads[c].start()
            share(h.at[chip, :, mine], h.at[chip, :, mine], len(GROUPS))
            for q in range(NQ):
                rows = slice(q * Q, (q + 1) * Q)
                lanes = lax.broadcasted_iota(jnp.int32, (Q, VBLK), 1) + v * WIDTH
                ids[rows, :] = jnp.broadcast_to(ids_flat[q:q + 1, :], (VBLK, Q)).T - lanes
                keeps[rows, :] = jnp.broadcast_to(bits_flat[q:q + 1, :], (VBLK, Q)).T
            wait_rows(ROWS, share_recv.at[len(GROUPS)])
            product(0, ROWS, (OWN,), first=True)
        elif step[0] == "got":
            group = GROUP_OF[step[1][0]]
            wait_rows(sum(n for _, _, n in step[1]), recv_sem.at[group])
            for c, r0, n in step[1]:
                part = h.at[slot[c], pl.ds(r0, n), mine]
                share(part, part, group)
        elif step[0] == "mul":
            product(*step[1:])
        else:
            last_product(step[1], pending)
            pending = sums(step[1])
    for last_step in pending:
        last_step()

    for p in peers:
        pltpu.make_async_remote_copy(
            src_ref=stats.at[v], dst_ref=stats.at[v], send_sem=stat_send, recv_sem=stat_recv,
            device_id={"vocab": p}, device_id_type=MESH,
        ).start()
    others = stats.at[0:N_VOCAB - 1]
    pltpu.make_async_copy(others, others, stat_recv).wait()
    picked = stats[0, 2]
    for d in range(1, N_VOCAB):
        picked += stats[d, 2]
    full = picked - lse_of(0)
    kept = picked - lse_of(1)
    out[0:NQ, :] = full
    out[NQ:2 * NQ, :] = kept
    gap = jnp.sum(kept - full, axis=0, keepdims=True)
    gaps[r] = jnp.broadcast_to(gap, (8, Q))
    for p in row_peers:
        pltpu.make_async_remote_copy(
            src_ref=gaps.at[r], dst_ref=gaps.at[r],
            send_sem=gap_send, recv_sem=gap_recv,
            device_id={"rows": p}, device_id_type=MESH,
        ).start()
    everyone = h.at[:, pl.ds(0, ROWS * 15 // 16), :]
    pltpu.make_async_copy(everyone, everyone, send_sem).wait()
    pltpu.make_async_copy(others, others, stat_send).wait()
    others = gaps.at[0:N_ROWS - 1]
    pltpu.make_async_copy(others, others, gap_recv).wait()
    everything = gaps[0]
    for i in range(1, N_ROWS):
        everything += gaps[i]
    lane = lax.broadcasted_iota(jnp.int32, (NQ, Q), 0)
    out[2 * NQ:, :] = jnp.where(lane == 0, everything[0:NQ] / TOKENS, 0.0)
    pltpu.make_async_copy(others, others, gap_send).wait()


def per_device(hidden, weights, sampled, keep_bits):
    anywhere = pl.BlockSpec(memory_space=pl.ANY)
    vmem = pl.BlockSpec(memory_space=pltpu.VMEM)
    dma = pltpu.SemaphoreType.DMA
    out = pl.pallas_call(
        kernel,
        out_shape=jax.ShapeDtypeStruct((3 * NQ, Q), F32),
        in_specs=[anywhere] * 4,
        out_specs=vmem,
        scratch_shapes=[
            pltpu.VMEM((CHIPS, ROWS, CHIP_FEAT), jnp.bfloat16),
            pltpu.VMEM((CHIPS, CHIP_FEAT, WIDTH), jnp.bfloat16),
            pltpu.VMEM((ROWS, WIDTH), F32),
            pltpu.VMEM((NQ, Q), jnp.int32),
            pltpu.VMEM((NQ, Q), jnp.int32),
            pltpu.VMEM((ROWS, VBLK), jnp.int32),
            pltpu.VMEM((ROWS, VBLK), jnp.int32),
            pltpu.VMEM((ROWS, VBLK), F32),
            pltpu.VMEM((ROWS, VBLK), F32),
            pltpu.VMEM((ROWS, VBLK), F32),
            pltpu.VMEM((ROWS, VBLK), F32),
            pltpu.VMEM((ROWS, VBLK), F32),
            pltpu.VMEM((N_VOCAB, 3, NQ, Q), F32),
            pltpu.VMEM((N_ROWS, 8, Q), F32),
            dma((3,)),
            dma((CHIPS,)),
            dma,
            dma((len(GROUPS),)),
            dma((len(GROUPS) + 1,)),
            dma,
            dma,
            dma,
            dma,
        ],
        compiler_params=pltpu.CompilerParams(
            collective_id=0, has_side_effects=True, vmem_limit_bytes=56 << 20
        ),
        cost_estimate=pl.CostEstimate(
            flops=2 * ROWS * WIDTH * CHIPS * CHIP_FEAT,
            bytes_accessed=2 * CHIPS * CHIP_FEAT * WIDTH,
            transcendentals=2 * ROWS * WIDTH,
        ),
    )(hidden, weights, sampled.reshape(NQ, Q), keep_bits.reshape(NQ, Q))
    out = out.reshape(3, ROWS)
    return out[0], out[1], jnp.sum(out[2])


def solution(mesh):
    placed = (P("rows", "vocab"), P(None, "vocab"), P("rows"), P("rows", "vocab"))
    return jax.shard_map(
        per_device,
        mesh=mesh,
        in_specs=placed,
        out_specs=(P("rows"), P("rows"), P()),
        check_vma=False,
    )
```
